32 devices in a mesh: dp: 4 (over y, x), tensor: 4 (over z), layers: 2 (over core).
Axes of the slice: x: 2, y: 2, z: 4, core: 2. Of those that a mesh axis runs over, the one named last changes fastest.
Arguments:
- section_input: bfloat16 [2, 512, 4096], P('layers', 'dp', 'tensor'), may hold values from -24 to 24
- out_cotangent: bfloat16 [512, 4096], P('dp', 'tensor'), may hold values from -24 to 24
- lift_weight: bfloat16 [2, 2048, 4096], P('layers', None, 'tensor'), may hold values from -0.125 to 0.125
- proj_weight: bfloat16 [2, 4096, 4096], P('layers', None, 'tensor'), may hold values from -0.09375 to 0.09375
- lift_mask: int32 [2, 16, 32], P('layers', None, 'tensor'), may hold values 0 or 1
- proj_mask: int32 [2, 32, 32], P('layers', None, 'tensor'), may hold values 0 or 1
- channel_perm: int32 [2, 4096], P('layers'), may hold values from 0 to 4095, each once within a row
- lift_moment: float32 [2, 2048, 4096], P('layers', 'dp', 'tensor'), may hold values from -3 to 3
- lift_square: float32 [2, 2048, 4096], P('layers', 'dp', 'tensor'), may hold values from 0.25 to 1
- proj_moment: float32 [2, 4096, 4096], P('layers', 'dp', 'tensor'), may hold values from -3 to 3
- proj_square: float32 [2, 4096, 4096], P('layers', 'dp', 'tensor'), may hold values from 0.25 to 1
Outputs:
- input_grad: float32 [2, 512, 4096], P('layers', 'dp', 'tensor')
- log_det: float32 [2], P('layers')
- lift_first: float32 [2, 2048, 4096], P('layers', 'dp', 'tensor')
- lift_second: float32 [2, 2048, 4096], P('layers', 'dp', 'tensor')
- lift_update: float32 [2, 2048, 4096], P('layers', 'dp', 'tensor')
- proj_first: float32 [2, 4096, 4096], P('layers', 'dp', 'tensor')
- proj_second: float32 [2, 4096, 4096], P('layers', 'dp', 'tensor')
- proj_update: float32 [2, 4096, 4096], P('layers', 'dp', 'tensor')
The draws below stay inside these ranges and needn't reach their ends.
Inputs may be any that keep to these rules, and one draw needn't show every extreme that they name: `channel_perm`: each row orders all 4096 features once. `lift_mask`: 1 keeps a block of 128 x 128 weights, 0 prunes it. `proj_mask`: 1 keeps a block of 128 x 128 weights, 0 prunes it.
All inputs are finite; a program needn't handle non-finite values.
Results may differ from the reference program's by a relative error of at most 0.008.
Values may be sent and summed in bfloat16 or wider, within the bound.
No kernel may reach another device: no remote copies, remote signals or barrier semaphores. Data moves between devices by JAX's collectives and lax.ppermute only.
A program may use at most 128 MiB of HBM per device.

```python
import jax
import jax.numpy as jnp
from jax import lax

FEAT = 4096
HID = 4096
BLK = 128
ADAM_STEP = 10
HALF = 2048
TOKENS = 512
CLIP = 4096
N_TENSOR = 4


def draw_out_cotangent(key, part):
    row_key, base_key = jax.random.split(key, 2)
    row_scale = jnp.exp(jax.random.uniform(row_key, (TOKENS, 1), jnp.float32, jnp.log(0.3), jnp.log(3.0)))
    col_scale = 0.6 * jnp.power(3.0, jnp.arange(FEAT, dtype=jnp.float32) / FEAT)[None, :]
    base_draw = jnp.clip(jax.random.normal(base_key, (TOKENS, FEAT), jnp.float32), -4.0, 4.0)
    return (row_scale * col_scale * base_draw).astype(jnp.bfloat16)


def draw_section_input(key, part):
    inner_key = jax.random.fold_in(key, 7)
    base_key = jax.random.fold_in(inner_key, 0)
    position = jnp.arange(TOKENS, dtype=jnp.float32)[None, :, None] / TOKENS
    row_scale = 0.3 * jnp.power(20.0, position)
    base_draw = jnp.clip(jax.random.normal(base_key, (2, TOKENS, FEAT), jnp.float32), -3.9, 3.9)
    return (row_scale * base_draw).astype(jnp.bfloat16)


def touch_ends(result, own_key, smallest, high):
    extent = result.shape
    index_at = [jax.random.randint(jax.random.fold_in(own_key, axis), (), 0, extent[axis]) for axis in range(len(extent))]
    result = result.at[tuple(index_at)].set(smallest)
    longest = extent.index(max(extent))
    index_at[longest] = (index_at[longest] + 1) % extent[longest]
    return result.at[tuple(index_at)].set(high)


def levels(key, dims, cuts, smallest, top_value):
    def one(dim, parts):
        heights = jax.random.uniform(jax.random.fold_in(jax.random.fold_in(key, 6), dim), (parts,), jnp.float32, smallest / len(cuts), top_value / len(cuts))
        return jnp.repeat(jnp.exp(heights), dims[dim] // parts).reshape((-1,) + (1,) * (len(dims) - dim - 1))

    factor_of = one(*cuts[0])
    for cut in cuts[1:]:
        factor_of = factor_of * one(*cut)
    return factor_of


def gaussian(rng, extent, scale, reach, pieces=(), held_as=jnp.bfloat16):
    loudness = levels(rng, extent, pieces, -0.22, 0.18) if pieces else 1.0
    entries = jax.random.normal(rng, extent, jnp.float32) * scale * loudness
    return jnp.minimum(jnp.maximum(entries, -reach), reach).astype(held_as)


def setup_inputs(seed: int = 0) -> dict:
    streams_of = jax.random.split(jax.random.key(seed), 12)
    return {
        "section_input": draw_section_input(jax.random.fold_in(streams_of[11], 71), 0),
        "out_cotangent": draw_out_cotangent(jax.random.fold_in(streams_of[11], 71), 0),
        "lift_weight": gaussian(streams_of[2], (2, HALF, HID), HALF ** -0.5, 0.125, ((0, 2), (2, 4))),
        "proj_weight": gaussian(streams_of[3], (2, 2 * HALF, HID), HID ** -0.5, 0.09375, ((0, 2), (2, 4))),
        "lift_mask": touch_ends((jax.random.randint(streams_of[4], (2, HALF // BLK, HID // BLK), 0, 2) < 1).astype(jnp.int32), jax.random.fold_in(streams_of[4], 1), 0, 1),
        "proj_mask": touch_ends((jax.random.randint(streams_of[5], (2, 2 * HALF // BLK, HID // BLK), 0, 2) < 1).astype(jnp.int32), jax.random.fold_in(streams_of[5], 1), 0, 1),
        "channel_perm": jax.vmap(lambda own: jax.random.permutation(own, FEAT))(jax.random.split(streams_of[6], 2)).reshape((2, FEAT)).astype(jnp.int32),
        "lift_moment": gaussian(streams_of[7], (2, HALF, HID), 0.5, 3.0, ((0, 2), (1, 4), (2, 4)), jnp.float32),
        "lift_square": jnp.clip(0.25 + 0.75 * jax.random.uniform(streams_of[8], (2, HALF, HID), jnp.float32) ** levels(streams_of[8], (2, HALF, HID), ((0, 2), (1, 4), (2, 4)), -0.2, 0.2), 0.25, 1.0),
        "proj_moment": gaussian(streams_of[9], (2, 2 * HALF, HID), 0.5, 3.0, ((0, 2), (1, 4), (2, 4)), jnp.float32),
        "proj_square": jnp.clip(0.25 + 0.75 * jax.random.uniform(streams_of[10], (2, 2 * HALF, HID), jnp.float32) ** levels(streams_of[10], (2, 2 * HALF, HID), ((0, 2), (1, 4), (2, 4)), -0.2, 0.2), 0.25, 1.0),
    }


beta_one = 0.9
beta_two = 0.99
adam_eps = 1e-08

def expand_blocks(block_mask):
    return jnp.repeat(jnp.repeat(block_mask, BLK, axis=0), BLK, axis=1) > 0

def shard_sum(left_mat, right_mat):
    part_width = left_mat.shape[1] // N_TENSOR
    running = jnp.zeros((left_mat.shape[0], right_mat.shape[0]), jnp.float32)
    for shard_idx in range(N_TENSOR):
        lo_col = shard_idx * part_width
        piece_sum = jnp.dot(left_mat[:, lo_col:lo_col + part_width], right_mat[:, lo_col:lo_col + part_width].T, preferred_element_type=jnp.float32)
        running = running + lax.optimization_barrier(piece_sum.astype(jnp.bfloat16)).astype(jnp.float32)
    return running

def section_grads(tokens, cotangent, lift_eff, proj_eff, channel_order):
    permuted = tokens[:, channel_order]
    cond_side = permuted[:, :HALF]
    moved_side = permuted[:, HALF:].astype(jnp.float32)
    pre_act = jnp.dot(cond_side, lift_eff, preferred_element_type=jnp.float32)
    hidden = jax.nn.silu(pre_act).astype(jnp.bfloat16)
    shared = shard_sum(hidden, proj_eff)
    raw_scale = shared[:, :HALF]
    shift_term = shared[:, HALF:]
    scale_term = jax.nn.sigmoid(raw_scale + 2.0)
    keep_part = 1.0 - scale_term
    log_mean = jnp.sum(jax.nn.log_sigmoid(raw_scale + 2.0)) / (TOKENS * HALF)
    grad_cond = cotangent[:, :HALF]
    grad_moved = cotangent[:, HALF:]
    grad_raw = grad_moved * (moved_side + shift_term) * scale_term * keep_part - keep_part
    grad_shift = grad_moved * scale_term
    grad_st = jnp.concatenate([grad_raw, grad_shift], axis=1).astype(jnp.bfloat16)
    grad_act = jnp.dot(grad_st, proj_eff, preferred_element_type=jnp.float32)
    squash = jax.nn.sigmoid(pre_act)
    grad_pre = (grad_act * squash * (1.0 + pre_act * (1.0 - squash))).astype(jnp.bfloat16)
    grad_inputs = grad_cond + shard_sum(grad_pre, lift_eff)
    grad_mixed = jnp.concatenate([grad_inputs, grad_shift], axis=1)
    inverse = jnp.zeros((FEAT,), jnp.int32).at[channel_order].set(jnp.arange(FEAT, dtype=jnp.int32))
    grad_in = grad_mixed[:, inverse]
    lift_grad = jnp.dot(cond_side.T, grad_pre, preferred_element_type=jnp.float32)
    proj_grad = jnp.dot(grad_st.T, hidden, preferred_element_type=jnp.float32)
    return (grad_in, log_mean, lift_grad, proj_grad)

def adam_step(gradient, kept, moment, square, factor):
    scaled = gradient * factor
    new_first = jnp.where(kept, beta_one * moment + (1.0 - beta_one) * scaled, moment)
    new_second = jnp.where(kept, beta_two * square + (1.0 - beta_two) * scaled * scaled, square)
    bias_one = 1.0 - beta_one ** ADAM_STEP
    bias_two = 1.0 - beta_two ** ADAM_STEP
    update = jnp.where(kept, new_first / bias_one / (jnp.sqrt(new_second / bias_two) + adam_eps), 0.0)
    return (new_first, new_second, update)

def reference(section_input, out_cotangent, lift_weight, proj_weight, lift_mask, proj_mask, channel_perm, lift_moment, lift_square, proj_moment, proj_square):
    cotangent = out_cotangent.astype(jnp.float32)
    grad_list = [None, None]
    log_list = [None, None]
    lift_grads = [None, None]
    proj_grads = [None, None]
    lift_keeps = [None, None]
    proj_keeps = [None, None]
    for section_idx in (1, 0):
        lift_keep = expand_blocks(lift_mask[section_idx])
        proj_keep = expand_blocks(proj_mask[section_idx])
        lift_eff = jnp.where(lift_keep, lift_weight[section_idx], jnp.zeros((), jnp.bfloat16))
        proj_eff = jnp.where(proj_keep, proj_weight[section_idx], jnp.zeros((), jnp.bfloat16))
        grad_in, log_mean, lift_grad, proj_grad = section_grads(section_input[section_idx], cotangent, lift_eff, proj_eff, channel_perm[section_idx])
        grad_list[section_idx] = grad_in
        log_list[section_idx] = log_mean
        lift_grads[section_idx] = jnp.where(lift_keep, lift_grad, 0.0)
        proj_grads[section_idx] = jnp.where(proj_keep, proj_grad, 0.0)
        lift_keeps[section_idx] = lift_keep
        proj_keeps[section_idx] = proj_keep
        cotangent = lax.optimization_barrier(grad_in.astype(jnp.bfloat16)).astype(jnp.float32)
    square_total = jnp.float32(0.0)
    for section_idx in (0, 1):
        square_total = square_total + jnp.sum(lift_grads[section_idx] * lift_grads[section_idx]) + jnp.sum(proj_grads[section_idx] * proj_grads[section_idx])
    factor = jnp.minimum(1.0, CLIP / (jnp.sqrt(square_total) + 1e-06))
    lift_out = [adam_step(lift_grads[s], lift_keeps[s], lift_moment[s], lift_square[s], factor) for s in (0, 1)]
    proj_out = [adam_step(proj_grads[s], proj_keeps[s], proj_moment[s], proj_square[s], factor) for s in (0, 1)]
    input_grad = jnp.stack(grad_list)
    log_det = jnp.stack(log_list)
    return (input_grad, log_det, jnp.stack([lift_out[0][0], lift_out[1][0]]), jnp.stack([lift_out[0][1], lift_out[1][1]]), jnp.stack([lift_out[0][2], lift_out[1][2]]), jnp.stack([proj_out[0][0], proj_out[1][0]]), jnp.stack([proj_out[0][1], proj_out[1][1]]), jnp.stack([proj_out[0][2], proj_out[1][2]]))
```

```python
import jax
import jax.numpy as jnp
from jax import lax
from jax.experimental import pallas as pl
from jax.experimental.pallas import tpu as pltpu
from jax.sharding import PartitionSpec as P

BLK = 128
ADAM_STEP = 10
CLIP = 4096

beta_one = 0.9
beta_two = 0.99
adam_eps = 1e-08

BF = jnp.bfloat16
F32 = jnp.float32
VMEM_LIMIT = 16 * 1024 * 1024


def vspec():
    return pl.BlockSpec(memory_space=pltpu.VMEM)


def sspec():
    return pl.BlockSpec(memory_space=pltpu.SMEM)


def params():
    return pltpu.CompilerParams(vmem_limit_bytes=VMEM_LIMIT)


def dot_nn(a, b):
    return lax.dot_general(a, b, (((1,), (0,)), ((), ())), preferred_element_type=F32)


def dot_nt(a, b):
    return lax.dot_general(a, b, (((1,), (1,)), ((), ())), preferred_element_type=F32)


def dot_tn(a, b):
    return lax.dot_general(a, b, (((0,), (0,)), ((), ())), preferred_element_type=F32)


def sigmoid(x):
    return 1.0 / (1.0 + jnp.exp(-x))


def xor_pairs(n, k):
    return [(i, i ^ k) for i in range(n)]


def over_tensor(x, pairs, layer):
    n_layers = lax.axis_size("layers")
    layers = range(n_layers) if layer is None else (layer,)
    route = [(a * n_layers + s, b * n_layers + s) for a, b in pairs for s in layers]
    return lax.ppermute(x, ("tensor", "layers"), route)


def over_dp(x, pairs, layer):
    n_layers = lax.axis_size("layers")
    layers = range(n_layers) if layer is None else (layer,)
    route = [(a * n_layers + s, b * n_layers + s) for a, b in pairs for s in layers]
    return lax.ppermute(x, ("dp", "layers"), route)


def scatter_tensor(chunks, layer):
    n = lax.axis_size("tensor")
    got = {k: over_tensor(chunks[k], xor_pairs(n, k), layer) for k in far_first(n)}
    return [chunks[0]] + [got[k] for k in range(1, n)]


def gather_tensor(x, layer):
    return scatter_tensor([x] * lax.axis_size("tensor"), layer)


def far_first(n):
    return sorted(range(1, n), key=lambda k: k < n // 2)


def scatter_dp(chunks, layer):
    n = lax.axis_size("dp")
    got = {k: over_dp(chunks[k], xor_pairs(n, k), layer) for k in reversed(range(1, n))}
    return [chunks[0]] + [got[k] for k in range(1, n)]


def down_a_section(chunks):
    n = lax.axis_size("tensor")
    m = lax.axis_size("layers")
    got = {
        k: lax.ppermute(
            chunks[k], ("tensor", "layers"), [(i * m + 1, j * m) for i, j in xor_pairs(n, k)]
        )
        for k in far_first(n)
    }
    got[0] = lax.ppermute(chunks[0], "layers", [(1, 0)])
    return [got[k] for k in range(n)]


def spread_halves(low, high, tensor_index):
    n = lax.axis_size("tensor")
    early = tensor_index < n // 2
    one = over_tensor(
        jnp.where(early, low, high),
        [(i, 2 * i if i < n // 2 else 2 * i + 1 - n) for i in range(n)],
        1,
    )
    two = over_tensor(
        jnp.where(early, high, low),
        [(i, 2 * i + 1 if i < n // 2 else 2 * i - n) for i in range(n)],
        1,
    )
    even = tensor_index % 2 == 0
    return jnp.where(even, one, two), jnp.where(even, two, one)


def whole(body, name, ins, outs, scratch=(), deps=()):
    arrays = [in_hbm(x) if m == pltpu.HBM else x for x, m in ins]
    specs = [pl.BlockSpec(memory_space=m) for _, m in ins]
    n_in, n_dep = len(arrays), len(deps)

    def run(*refs):
        body(*refs[:n_in], *refs[n_in + n_dep :])

    return pl.pallas_call(
        run,
        in_specs=specs + [pl.BlockSpec(memory_space=pl.ANY)] * n_dep,
        out_specs=[vspec()] * len(outs),
        out_shape=[jax.ShapeDtypeStruct(s, d) for s, d in outs],
        scratch_shapes=list(scratch),
        compiler_params=params(),
        name=name,
    )(*arrays, *deps)


def on_vmem(arrays):
    return [(x, pltpu.VMEM) for x in arrays]


def in_hbm(x):
    return pltpu.with_memory_space_constraint(x, pltpu.HBM)


def tile_width(width):
    return next(c for c in (512, 256, 128) if width % c == 0)


def tiles_of(width):
    tile = tile_width(width)
    return [slice(i, i + tile) for i in range(0, width, tile)]


def loads(src, dst, sems, count):
    rows = src.shape[0] // count
    return [
        pltpu.make_async_copy(
            src.at[pl.ds(c * rows, rows)], dst.at[pl.ds(c * rows, rows)], sems.at[c]
        )
        for c in range(count)
    ]


SPAN = 256


def span_of(size):
    return next(c for c in (SPAN, SPAN // 2) if size % c == 0)


def fill_hot(hot_s, at, row, base, span):
    width = row.shape[1]
    near = jnp.broadcast_to(row - base, (16, width)).astype(BF)
    step = lax.broadcasted_iota(jnp.int32, (16, width), 0).astype(F32)
    for i in range(0, span, 16):
        hit = (step + float(i)).astype(BF) == near
        hot_s[at + i : at + i + 16, :] = jnp.where(
            hit, jnp.ones((16, width), BF), jnp.zeros((16, width), BF)
        )


def prep_weights(lift_mask, proj_mask, lift, proj):
    steps = min(8, lift.shape[0] // BLK)

    def body(lift_mask_ref, proj_mask_ref, lift_ref, proj_ref, lift_out, proj_out):
        for mask, src, dst in (
            (lift_mask_ref, lift_ref, lift_out),
            (proj_mask_ref, proj_ref, proj_out),
        ):
            n_rows = src.shape[0] // BLK
            for r in range(n_rows):
                for c in range(src.shape[1] // BLK):
                    at = (slice(r * BLK, (r + 1) * BLK), slice(c * BLK, (c + 1) * BLK))
                    kept = mask[pl.program_id(0) * n_rows + r, c] > 0
                    tile = src[at]
                    dst[at] = jnp.where(kept, tile, jnp.zeros_like(tile))

    specs = [
        pl.BlockSpec((x.shape[0] // steps, x.shape[1]), lambda i: (i, 0)) for x in (lift, proj)
    ]
    return pl.pallas_call(
        body,
        grid=(steps,),
        in_specs=[sspec(), sspec()] + specs,
        out_specs=specs,
        out_shape=[pltpu.HBM(lift.shape, BF), pltpu.HBM(proj.shape, BF)],
        compiler_params=params(),
        name="prep_weights",
    )(lift_mask, proj_mask, in_hbm(lift), in_hbm(proj))


def prep_inverse(perm, feat, deps):
    width = perm.shape[1]
    tile = tile_width(width)
    span = span_of(feat)

    def body(perm_ref, inv_ref, hot_s):
        lane = lax.broadcasted_iota(jnp.int32, (16, tile), 1)
        which = lax.broadcasted_iota(jnp.int32, (16, tile), 0)

        def step(s, _):
            base = s * span
            acc = jnp.zeros((16, span), F32)
            for c in range(width // tile):
                fill_hot(
                    hot_s, 0, perm_ref[:, c * tile : (c + 1) * tile], base.astype(F32), span
                )
                place = lane + (c * tile + 1)
                value = jnp.where(which == 0, place // 64, jnp.where(which == 1, place % 64, 0))
                acc = acc + dot_nt(value.astype(F32).astype(BF), hot_s[...])
            inv = acc[0:1, :] * 64.0 + acc[1:2, :] - 1.0
            inv_ref[:, pl.ds(pl.multiple_of(base, span), span)] = inv
            return 0

        lax.fori_loop(0, feat // span, step, 0)

    return whole(
        body,
        "prep_inverse",
        on_vmem([perm]),
        [((1, feat), F32)],
        [pltpu.VMEM((span, tile), BF)],
        deps=deps,
    )[0]


def forward(idx, tokens, perm, lift, proj, n, deps):
    rows, block = tokens[0].shape
    width = perm.shape[1]
    half, hid = lift.shape
    hb = half // n
    tile = tile_width(width)
    span = span_of(block)

    def body(idx_ref, *refs):
        tok = refs[:n]
        perm_ref, lift_h, proj_h, slope_ref, perm_s, hidden_ref = refs[n : n + 6]
        shared_out = refs[n + 6 : n + 6 + n]
        hot_s, lift_ref, proj_ref, lift_sem, proj_sem = refs[-5:]
        t = idx_ref[0]
        lift_in = loads(lift_h, lift_ref, lift_sem, n)
        proj_in = loads(proj_h, proj_ref, proj_sem, 2 * n)
        for copy in lift_in + proj_in:
            copy.start()

        def columns(c, _):
            cols = pl.ds(pl.multiple_of(c * tile, tile), tile)
            row = perm_ref[:, cols]
            acc = jnp.zeros((rows, tile), F32)
            for k in range(n):
                for i in range(0, block, span):
                    base = ((t ^ k) * block + i).astype(F32)
                    fill_hot(hot_s.at[k % 2], i, row, base, span)
                acc = acc + dot_nn(tok[k][...], hot_s[k % 2])
            perm_s[:, cols] = acc.astype(BF)
            return 0

        lax.fori_loop(0, width // tile, columns, 0)
        for copy in lift_in:
            copy.wait()
        for cols in tiles_of(hid):
            pre = dot_nn(perm_s[:, :half], lift_ref[:, cols])
            squash = sigmoid(pre)
            hidden_ref[:, cols] = (pre * squash).astype(BF)
            slope_ref[:, cols] = squash * (1.0 + pre * (1.0 - squash))
        hidden = hidden_ref[...]
        for copy in proj_in:
            copy.wait()
        for k in range(n):
            at = pl.multiple_of((t ^ k) * hb, hb)
            shared_out[k][:, :hb] = dot_nt(hidden, proj_ref[pl.ds(at, hb), :]).astype(BF)
            shared_out[k][:, hb:] = dot_nt(hidden, proj_ref[pl.ds(half + at, hb), :]).astype(BF)

    outs = whole(
        body,
        "forward",
        [(idx, pltpu.SMEM)]
        + on_vmem(list(tokens) + [perm])
        + [(lift, pltpu.HBM), (proj, pltpu.HBM)],
        [((rows, hid), F32), ((rows, width), BF), ((rows, hid), BF)]
        + [((rows, 2 * hb), BF)] * n,
        [
            pltpu.VMEM((2, block, tile), BF),
            pltpu.VMEM(lift.shape, BF),
            pltpu.VMEM(proj.shape, BF),
            pltpu.SemaphoreType.DMA((n,)),
            pltpu.SemaphoreType.DMA((2 * n,)),
        ],
        deps=deps,
    )
    return outs[0], outs[1], outs[2], outs[3:]


def bundles(idx, columns, hidden, half, n_dp):
    rows, hid = hidden.shape
    dpc = half // n_dp

    def body(idx_ref, columns_ref, hidden_ref, *refs):
        out, cond_s = refs[:n_dp], refs[n_dp]

        @pl.when(idx_ref[1] == 0)
        def _():
            fill_bundle(out, 0, columns_ref, hidden_ref, cond_s, idx_ref[2])

    return whole(
        body,
        "bundles",
        [(idx, pltpu.SMEM)] + on_vmem([columns, hidden]),
        [((rows, hid + dpc), BF)] * n_dp,
        [pltpu.VMEM((n_dp, rows, dpc), BF)],
    )


def fill_bundle(out, at, columns_ref, hidden_ref, cond_s, d):
    n_dp, _, dpc = cond_s.shape
    hid = hidden_ref.shape[1]
    for j in range(n_dp):
        cond_s[j] = columns_ref[:, j * dpc : (j + 1) * dpc]
    for k in range(n_dp):
        out[k][:, at : at + hid] = hidden_ref[...]
        out[k][:, at + hid : at + hid + dpc] = cond_s[d ^ k]


def couple(chunks, columns, half, cot, deps):
    n = len(chunks)
    n_cot = len(cot)
    rows, two_hb = chunks[0].shape
    hb = two_hb // 2

    def body(*refs):
        parts = refs[:n]
        cots = refs[n : n + n_cot]
        columns_ref, st_ref, log_ref = refs[n + n_cot :]
        raw = parts[0][:, :hb].astype(F32)
        shift = parts[0][:, hb:].astype(F32)
        for k in range(1, n):
            raw = raw + parts[k][:, :hb].astype(F32)
            shift = shift + parts[k][:, hb:].astype(F32)
        arg = raw + 2.0
        scale = sigmoid(arg)
        keep = 1.0 - scale
        cot = cots[0][...].astype(F32)
        for c in cots[1:]:
            cot = cot + c[...].astype(F32)
        cot = cot.astype(BF).astype(F32)
        grad_raw = cot * (columns_ref[:, half:].astype(F32) + shift) * scale * keep - keep
        st_ref[:, :hb] = grad_raw.astype(BF)
        st_ref[:, hb:] = (cot * scale).astype(BF)
        logs = jnp.minimum(arg, 0.0) - jnp.log(1.0 + jnp.exp(-jnp.abs(arg)))
        log_ref[...] = jnp.sum(logs, axis=0, keepdims=True)

    return whole(
        body,
        "couple",
        on_vmem(list(chunks) + list(cot) + [columns]),
        [((rows, two_hb), BF), ((1, hb), F32)],
        deps=deps,
    )


def fill_pack(pack, st_s, d, n_dp, m, hid, hb):
    for j in range(n_dp):
        for i in range(m):
            pack[j][:, hid + i * hb : hid + (i + 1) * hb] = st_s[(d ^ j) * m + i]


def order_st(st_ref, st_s, t, n, hb):
    for k in range(n):
        st_s[t ^ k] = st_ref[k][:, :hb]
        st_s[n + (t ^ k)] = st_ref[k][:, hb:]


def hidden_cotangent(st_s, slope_ref, proj_in, proj_ref, out_ref, n, hb, hid):
    for cols in tiles_of(hid):
        acc = None
        for k in range(2 * n):
            if cols.start == 0:
                proj_in[k].wait()
            part = dot_nn(st_s[k], proj_ref[k * hb : (k + 1) * hb, cols])
            acc = part if acc is None else acc + part
        out_ref[:, cols] = (acc * slope_ref[:, cols]).astype(BF)


def mixed_part(pre, extra, shift_cot, lift_ref, part_s, n, hb):
    for b in range(n):
        part = dot_nt(pre, lift_ref[b * hb : (b + 1) * hb, :])
        part_s[:, b * hb : (b + 1) * hb] = (part + extra(b)).astype(BF)
    part_s[:, n * hb :] = shift_cot


def natural_columns(part_ref, inv_ref, hot_s, first, count, hb, store):
    width = part_ref.shape[1]
    span = span_of(width)

    def one(q, _):
        row = inv_ref[:, pl.ds(pl.multiple_of(q * hb, hb), hb)]
        for i in range(0, width, span):
            fill_hot(hot_s, i, row, float(i), span)
        store(q, dot_nn(part_ref[...], hot_s[...]).astype(BF))
        return 0

    lax.fori_loop(first, first + count, one, 0)


def backward_one(idx, st, ca, slope, inv, lift, proj, width, n):
    rows, two_hb = st[0].shape
    hb = two_hb // 2
    hid = lift.shape[1]

    def body(idx_ref, *refs):
        st_ref = refs[:n]
        ca_ref, slope_ref, inv_ref, lift_h, proj_h = refs[n : n + 5]
        pre_ref, part_ref, nat_ref = refs[n + 5 : n + 8]
        second_out = refs[n + 8 : 2 * n + 8]
        st_s, hot_s, lift_ref, proj_ref, lift_sem, proj_sem = refs[-6:]
        t = idx_ref[0]
        proj_in = loads(proj_h, proj_ref, proj_sem, 2 * n)
        lift_in = loads(lift_h, lift_ref, lift_sem, n)
        for copy in proj_in + lift_in:
            copy.start()
        order_st(st_ref, st_s, t, n, hb)
        hidden_cotangent(st_s, slope_ref, proj_in, proj_ref, pre_ref, n, hb, hid)
        for copy in lift_in:
            copy.wait()
        mixed_part(
            pre_ref[...], lambda b: jnp.where(t == b, ca_ref[...].astype(F32), 0.0),
            st_ref[0][:, hb:], lift_ref, part_ref, n, hb,
        )

        def store(q, block):
            nat_ref[q - n] = block

        natural_columns(part_ref, inv_ref, hot_s, n, n, hb, store)
        for k in range(n):
            second_out[k][...] = nat_ref[t ^ k]

    outs = whole(
        body,
        "backward_one",
        [(idx, pltpu.SMEM)]
        + on_vmem(list(st) + [ca, slope, inv])
        + [(lift, pltpu.HBM), (proj, pltpu.HBM)],
        [((rows, hid), BF), ((rows, width), BF), ((n, rows, hb), BF)] + [((rows, hb), BF)] * n,
        [
            pltpu.VMEM((2 * n, rows, hb), BF),
            pltpu.VMEM((width, hb), BF),
            pltpu.VMEM(lift.shape, BF),
            pltpu.VMEM(proj.shape, BF),
            pltpu.SemaphoreType.DMA((n,)),
            pltpu.SemaphoreType.DMA((2 * n,)),
        ],
    )
    return outs[0], outs[1], outs[2], outs[3:]


def packs_one(idx, st, pre, columns, hidden, half, n_dp, deps):
    n = len(st)
    rows, two_hb = st[0].shape
    hb = two_hb // 2
    hid = pre.shape[1]
    m = 2 * n // n_dp
    dpc = half // n_dp

    def body(idx_ref, *refs):
        st_ref = refs[:n]
        pre_ref, columns_ref, hidden_ref = refs[n : n + 3]
        pack = refs[n + 3 : n + 3 + n_dp]
        st_s, cond_s = refs[-2:]

        @pl.when(idx_ref[1] != 0)
        def _():
            order_st(st_ref, st_s, idx_ref[0], n, hb)
            for j in range(n_dp):
                pack[j][:, :hid] = pre_ref[...]
            fill_pack(pack, st_s, idx_ref[2], n_dp, m, hid, hb)
            fill_bundle(pack, hid + m * hb, columns_ref, hidden_ref, cond_s, idx_ref[2])

    return whole(
        body,
        "packs_one",
        [(idx, pltpu.SMEM)] + on_vmem(list(st) + [pre, columns, hidden]),
        [((rows, 2 * hid + m * hb + dpc), BF)] * n_dp,
        [pltpu.VMEM((2 * n, rows, hb), BF), pltpu.VMEM((n_dp, rows, dpc), BF)],
        deps=deps,
    )


def backward_one_rest(idx, part, inv, n, deps):
    rows, width = part.shape
    hb = inv.shape[1] // (2 * n)

    def body(idx_ref, part_ref, inv_ref, nat_ref, hot_s):
        @pl.when(idx_ref[1] != 0)
        def _():
            def store(q, block):
                nat_ref[q] = block

            natural_columns(part_ref, inv_ref, hot_s, 0, n, hb, store)

    return whole(
        body,
        "backward_one_rest",
        [(idx, pltpu.SMEM)] + on_vmem([part, inv]),
        [((n, rows, hb), BF)],
        [pltpu.VMEM((width, hb), BF)],
        deps=deps,
    )[0]


def chunks_of(idx, stack, deps):
    n, rows, cols = stack.shape[0] // 2, stack.shape[1], stack.shape[2]

    def body(idx_ref, stack_ref, *out):
        for k in range(n):
            for i in range(2):
                out[k][:, i * cols : (i + 1) * cols] = stack_ref[2 * (idx_ref[0] ^ k) + i]

    return whole(
        body,
        "chunks_of",
        [(idx, pltpu.SMEM)] + on_vmem([stack]),
        [((rows, 2 * cols), BF)] * n,
        deps=deps,
    )


def backward_zero(idx, st, slope, proj, n, n_dp, deps):
    rows, two_hb = st[0].shape
    hb = two_hb // 2
    hid = proj.shape[1]
    m = 2 * n // n_dp

    def body(idx_ref, *refs):
        st_ref = refs[:n]
        slope_ref, proj_h = refs[n : n + 2]
        pack = refs[n + 2 : n + 2 + n_dp]
        st_s, proj_ref, proj_sem = refs[-3:]

        @pl.when(idx_ref[1] == 0)
        def _():
            proj_in = loads(proj_h, proj_ref, proj_sem, 2 * n)
            for copy in proj_in:
                copy.start()
            order_st(st_ref, st_s, idx_ref[0], n, hb)
            hidden_cotangent(st_s, slope_ref, proj_in, proj_ref, pack[0], n, hb, hid)
            for j in range(1, n_dp):
                pack[j][:, :hid] = pack[0][:, :hid]
            fill_pack(pack, st_s, idx_ref[2], n_dp, m, hid, hb)

    return whole(
        body,
        "backward_zero",
        [(idx, pltpu.SMEM)] + on_vmem(list(st) + [slope]) + [(proj, pltpu.HBM)],
        [((rows, hid + m * hb), BF)] * n_dp,
        [
            pltpu.VMEM((2 * n, rows, hb), BF),
            pltpu.VMEM(proj.shape, BF),
            pltpu.SemaphoreType.DMA((2 * n,)),
        ],
        deps=deps,
    )


def natural_shares(idx, st_own, pack, low_one, inv, lift, low, high, width, n):
    rows, two_hb = st_own.shape
    hb = two_hb // 2
    hid = lift.shape[1]

    def body(idx_ref, st_ref, pack_ref, *refs):
        got_ref, inv_ref, lift_h, low_ref, high_ref, nat_s, part_s, hot_s, lift_ref, lift_sem = refs

        @pl.when(idx_ref[1] == 0)
        def _():
            lift_in = loads(lift_h, lift_ref, lift_sem, n)
            for copy in lift_in:
                copy.start()
            for copy in lift_in:
                copy.wait()
            mixed_part(
                pack_ref[:, :hid], lambda b: got_ref[b].astype(F32), st_ref[:, hb:], lift_ref,
                part_s, n, hb,
            )

            def store(q, block):
                nat_s[q] = block

            natural_columns(part_s, inv_ref, hot_s, 0, 2 * n, hb, store)

        @pl.when(idx_ref[1] != 0)
        def _():
            for q in range(n):
                nat_s[q] = low_ref[q]
                nat_s[n + q] = high_ref[q]

    return whole(
        body,
        "natural_shares",
        [(idx, pltpu.SMEM)]
        + on_vmem([st_own, pack, low_one, inv])
        + [(lift, pltpu.HBM)]
        + on_vmem([low, high]),
        [((2 * n, rows, hb), BF)],
        [
            pltpu.VMEM((rows, width), BF),
            pltpu.VMEM((width, hb), BF),
            pltpu.VMEM(lift.shape, BF),
            pltpu.SemaphoreType.DMA((n,)),
        ],
    )[0]


def fetch(idx_ref, kind, bund, zero, one, lhs, rhs, sem, wait):
    n_dp = len(one)
    rows = one[0].shape[0]
    hid = rhs.shape[1]
    width = lhs.shape[1]
    st_cols = zero[0].shape[1] - hid

    def act(src, first, dst, k, of):
        copy = pltpu.make_async_copy(
            src.at[:, pl.ds(first, dst.shape[1])],
            dst.at[pl.ds(k * rows, rows)],
            sem.at[of * n_dp + k],
        )
        if wait:
            copy.wait()
        else:
            copy.start()

    def act_all(pack, late, late_at):
        for k in range(n_dp):
            if kind == "proj":
                act(pack[k], hid, lhs, k, 0)
                act(late[k], late_at, rhs, k, 1)
            else:
                act(late[k], late_at + hid, lhs, k, 0)
                act(pack[k], 0, rhs, k, 1)

    @pl.when(idx_ref[1] == 0)
    def _():
        act_all(zero, bund, 0)

    @pl.when(idx_ref[1] != 0)
    def _():
        act_all(one, one, hid + st_cols)


def factors(kind, bund, zero, hid):
    n_dp = len(zero)
    tokens = n_dp * zero[0].shape[0]
    width = (zero if kind == "proj" else bund)[0].shape[1] - hid
    return [
        pltpu.VMEM((tokens, width), BF),
        pltpu.VMEM((tokens, hid), BF),
        pltpu.SemaphoreType.DMA((2 * n_dp,)),
    ]


def weight_squares(idx, lift_mask, proj_mask, bund, zero, one, logs, hid):
    n_dp = len(zero)
    lift_s = factors("lift", bund, zero, hid)
    proj_s = factors("proj", bund, zero, hid)

    def body(idx_ref, lift_mask_ref, proj_mask_ref, log_ref, *refs):
        packs = [refs[i * n_dp : (i + 1) * n_dp] for i in range(3)]
        refs = refs[3 * n_dp :]
        sum_ref, sq_s = refs[:2]
        groups = (("proj", proj_mask_ref, refs[2:5]), ("lift", lift_mask_ref, refs[5:8]))
        for wait in (False, True):
            for kind, _, (lhs, rhs, sem) in groups:
                fetch(idx_ref, kind, *packs, lhs, rhs, sem, wait)
        sq_s[...] = jnp.zeros_like(sq_s)
        d = idx_ref[2]
        for kind, mask, (lhs, rhs, _) in groups:
            n_rows = lhs.shape[1]
            first = d * (n_rows // BLK)
            tile = min(512, n_rows)
            for cols in tiles_of(hid):
                for r in range(0, n_rows, tile):
                    grad = dot_tn(lhs[:, r : r + tile], rhs[:, cols])
                    total = None
                    for i in range(grad.shape[0] // BLK):
                        for j in range(grad.shape[1] // BLK):
                            part = grad[i * BLK : (i + 1) * BLK, j * BLK : (j + 1) * BLK]
                            kept = mask[first + r // BLK + i, cols.start // BLK + j] > 0
                            part = jnp.sum((part * part).reshape(BLK // 8, 8, BLK), axis=0)
                            part = jnp.where(kept, part, 0.0)
                            total = part if total is None else total + part
                    sq_s[...] += total
        lane = lax.broadcasted_iota(jnp.int32, sum_ref.shape, 1)
        square = jnp.sum(sq_s[...])
        log_sum = jnp.sum(log_ref[...])
        sum_ref[...] = jnp.where(lane == 0, square, jnp.where(lane == 1, log_sum, 0.0))

    n_all = lax.axis_size("dp") * lax.axis_size("tensor") * lax.axis_size("layers")
    return whole(
        body,
        "weight_squares",
        [(idx, pltpu.SMEM), (lift_mask, pltpu.SMEM), (proj_mask, pltpu.SMEM), (logs, pltpu.VMEM)]
        + [(x, pltpu.HBM) for x in list(bund) + list(zero) + list(one)],
        [((n_all, BLK), F32)],
        [pltpu.VMEM((8, BLK), F32)] + proj_s + lift_s,
    )[0]


def adam(idx, sums, kind, mask, bund, zero, one, moment, square, hid, dep):
    n_dp = len(zero)
    n_rows, n_cols = moment.shape
    tile = min(256, n_rows)
    inv_one = 1.0 / (1.0 - beta_one**ADAM_STEP)
    inv_two = 1.0 / (1.0 - beta_two**ADAM_STEP)

    def body(idx_ref, mask_ref, sums_ref, dep_ref, *refs):
        packs = [refs[i * n_dp : (i + 1) * n_dp] for i in range(3)]
        m_ref, v_ref, first_ref, second_ref, upd_ref, lhs, rhs, sem = refs[3 * n_dp :]
        step = pl.program_id(0)

        @pl.when(step == 0)
        def _():
            for wait in (False, True):
                fetch(idx_ref, kind, *packs, lhs, rhs, sem, wait)

        row = idx_ref[2] * (n_rows // BLK) + step * (tile // BLK)
        square_total = jnp.sum(sums_ref[:, 0:1], axis=0, keepdims=True)
        factor = jnp.minimum(1.0, CLIP / (jnp.sqrt(square_total) + 1e-06))
        left = lhs[:, pl.ds(pl.multiple_of(step * tile, tile), tile)]
        for cols in tiles_of(n_cols):
            grad = dot_tn(left, rhs[:, cols])
            for i in range(tile // BLK):
                for j in range(grad.shape[1] // BLK):
                    at = (
                        slice(i * BLK, (i + 1) * BLK),
                        slice(cols.start + j * BLK, cols.start + (j + 1) * BLK),
                    )
                    kept = mask_ref[row + i, cols.start // BLK + j] > 0
                    g = grad[i * BLK : (i + 1) * BLK, j * BLK : (j + 1) * BLK] * factor
                    old_m, old_v = m_ref[at], v_ref[at]
                    new_m = jnp.where(kept, beta_one * old_m + (1.0 - beta_one) * g, old_m)
                    new_v = jnp.where(kept, beta_two * old_v + (1.0 - beta_two) * g * g, old_v)
                    spread = new_v * inv_two
                    upd = (new_m * inv_one) / (spread * lax.rsqrt(spread) + adam_eps)
                    first_ref[at] = new_m
                    second_ref[at] = new_v
                    upd_ref[at] = jnp.where(kept, upd, 0.0)

    spec = pl.BlockSpec((tile, n_cols), lambda i: (i, 0))
    return pl.pallas_call(
        body,
        grid=(n_rows // tile,),
        in_specs=[sspec()] * 2
        + [vspec()]
        + [pl.BlockSpec(memory_space=pl.ANY)]
        + [pl.BlockSpec(memory_space=pltpu.HBM)] * (3 * n_dp)
        + [spec] * 2,
        out_specs=[spec] * 3,
        out_shape=[pltpu.HBM(moment.shape, F32)] * 3,
        scratch_shapes=factors(kind, bund, zero, hid),
        compiler_params=pltpu.CompilerParams(vmem_limit_bytes=VMEM_LIMIT),
        name="adam_" + kind,
    )(
        idx, mask, sums, dep, *map(in_hbm, (*bund, *zero, *one)), in_hbm(moment), in_hbm(square)
    )


def total(parts):
    acc = parts[0].astype(F32)
    for p in parts[1:]:
        acc = acc + p.astype(F32)
    return acc


def per_device(
    section_input,
    out_cotangent,
    lift_weight,
    proj_weight,
    lift_mask,
    proj_mask,
    channel_perm,
    lift_moment,
    lift_square,
    proj_moment,
    proj_square,
):
    n = lax.axis_size("tensor")
    n_dp = lax.axis_size("dp")
    t = lax.axis_index("tensor")
    section = lax.axis_index("layers")
    d = lax.axis_index("dp")
    idx = jnp.stack([t, section, d]).astype(jnp.int32)
    perm = channel_perm[0]
    feat = perm.shape[0]
    half = feat // 2
    hb = half // n
    rows = section_input.shape[1]
    lift_mask, proj_mask = lift_mask[0], proj_mask[0]

    with jax.named_scope("tokens_exchange"):
        tokens = gather_tensor(section_input[0], None)
    with jax.named_scope("cotangent_exchange"):
        ca, cb = spread_halves(out_cotangent[:, :hb], out_cotangent[:, hb:], t)

    own = lax.dynamic_slice_in_dim(perm, half + t * hb, hb, 0)
    perm_cols = jnp.concatenate([perm[:half], own])[None].astype(F32)
    width = perm_cols.shape[1]
    lift, proj = prep_weights(lift_mask, proj_mask, lift_weight[0], proj_weight[0])
    hid = lift.shape[1]

    slope, columns, hidden, shared = forward(
        idx, tokens, perm_cols, lift, proj, n, (ca, cb)
    )
    with jax.named_scope("shared_exchange"):
        shared = scatter_tensor(shared, None)
    with jax.named_scope("hidden_exchange"):
        bund = scatter_dp(bundles(idx, columns, hidden, half, n_dp), 0)
    inv = prep_inverse(perm_cols, feat, (columns,))

    st_own, logs = couple(shared, columns, half, [cb], (inv,) + tuple(bund[1:]))
    with jax.named_scope("st_one_exchange"):
        st = gather_tensor(st_own, 1)
    pre, part, high, second = backward_one(idx, st, ca, slope, inv, lift, proj, width, n)
    with jax.named_scope("down_exchange"):
        cb_zero = down_a_section(second)

    st_own, _ = couple(shared, columns, half, cb_zero, ())
    with jax.named_scope("st_zero_exchange"):
        st_zero = gather_tensor(st_own, 0)
    pack_one = packs_one(idx, st, pre, columns, hidden, half, n_dp, tuple(st_zero))
    with jax.named_scope("dp_one_exchange"):
        pack_one = scatter_dp(pack_one, 1)
    low = backward_one_rest(idx, part, inv, n, tuple(pack_one[1:]))
    with jax.named_scope("down_late_exchange"):
        low_one = lax.ppermute(low, "layers", [(1, 0)])
    pack_zero = backward_zero(idx, st_zero, slope, proj, n, n_dp, ())
    with jax.named_scope("dp_zero_exchange"):
        pack_got = scatter_dp(pack_zero, 0)
    shares = natural_shares(
        idx, st_own, pack_zero[0], low_one, inv, lift, low, high, width, n
    )

    sources = (bund, pack_got, pack_one)
    sums = weight_squares(idx, lift_mask, proj_mask, *sources, logs, hid)
    with jax.named_scope("norm_exchange"):
        sums = lax.all_to_all(
            sums, ("dp", "tensor", "layers"), split_axis=0, concat_axis=0, tiled=True
        )
    shares = chunks_of(idx, shares, (sums,))
    lift_out = adam(
        idx, sums, "lift", lift_mask, *sources, lift_moment[0], lift_square[0], hid, shares[0]
    )
    with jax.named_scope("input_exchange"):
        shares = scatter_tensor(shares, None)
    proj_out = adam(
        idx, sums, "proj", proj_mask, *sources, proj_moment[0], proj_square[0], hid, shares[0]
    )

    input_grad = total(shares)[None]
    by_section = sums.reshape(n_dp * n, -1, BLK)
    log_total = jnp.sum(lax.dynamic_index_in_dim(by_section, section, 1, False)[:, 1])
    log_det = (log_total / (rows * n_dp * half)).reshape(1)
    return (
        input_grad,
        log_det,
        lift_out[0][None],
        lift_out[1][None],
        lift_out[2][None],
        proj_out[0][None],
        proj_out[1][None],
        proj_out[2][None],
    )


def solution(mesh):
    return jax.shard_map(
        per_device,
        mesh=mesh,
        in_specs=(
            P("layers", "dp", "tensor"),
            P("dp", "tensor"),
            P("layers", None, "tensor"),
            P("layers", None, "tensor"),
            P("layers", None, "tensor"),
            P("layers", None, "tensor"),
            P("layers", None),
            P("layers", "dp", "tensor"),
            P("layers", "dp", "tensor"),
            P("layers", "dp", "tensor"),
            P("layers", "dp", "tensor"),
        ),
        out_specs=(
            P("layers", "dp", "tensor"),
            P("layers"),
            P("layers", "dp", "tensor"),
            P("layers", "dp", "tensor"),
            P("layers", "dp", "tensor"),
            P("layers", "dp", "tensor"),
            P("layers", "dp", "tensor"),
            P("layers", "dp", "tensor"),
        ),
        check_vma=False,
    )
```

```python
import jax
import jax.numpy as jnp
from jax import lax
from jax.experimental import pallas as pl
from jax.experimental.pallas import tpu as pltpu
from jax.sharding import PartitionSpec as P

BLK = 128
ADAM_STEP = 10
CLIP = 4096

beta_one = 0.9
beta_two = 0.99
adam_eps = 1e-08

BF = jnp.bfloat16
F32 = jnp.float32
VMEM_LIMIT = 16 * 1024 * 1024


def vspec():
    return pl.BlockSpec(memory_space=pltpu.VMEM)


def sspec():
    return pl.BlockSpec(memory_space=pltpu.SMEM)


def params():
    return pltpu.CompilerParams(vmem_limit_bytes=VMEM_LIMIT)


def dot_nn(a, b):
    return lax.dot_general(a, b, (((1,), (0,)), ((), ())), preferred_element_type=F32)


def dot_nt(a, b):
    return lax.dot_general(a, b, (((1,), (1,)), ((), ())), preferred_element_type=F32)


def dot_tn(a, b):
    return lax.dot_general(a, b, (((0,), (0,)), ((), ())), preferred_element_type=F32)


def sigmoid(x):
    return 1.0 / (1.0 + jnp.exp(-x))


def xor_pairs(n, k):
    return [(i, i ^ k) for i in range(n)]


def over_tensor(x, pairs, layer):
    n_layers = lax.axis_size("layers")
    layers = range(n_layers) if layer is None else (layer,)
    route = [(a * n_layers + s, b * n_layers + s) for a, b in pairs for s in layers]
    return lax.ppermute(x, ("tensor", "layers"), route)


def over_dp(x, pairs, layer):
    n_layers = lax.axis_size("layers")
    layers = range(n_layers) if layer is None else (layer,)
    route = [(a * n_layers + s, b * n_layers + s) for a, b in pairs for s in layers]
    return lax.ppermute(x, ("dp", "layers"), route)


def scatter_tensor(chunks, layer):
    n = lax.axis_size("tensor")
    got = {k: over_tensor(chunks[k], xor_pairs(n, k), layer) for k in far_first(n)}
    return [chunks[0]] + [got[k] for k in range(1, n)]


def gather_tensor(x, layer):
    n = lax.axis_size("tensor")
    got = {k: over_tensor(x, xor_pairs(n, k), layer) for k in reversed(far_first(n))}
    return [x] + [got[k] for k in range(1, n)]


def far_first(n):
    return sorted(range(1, n), key=lambda k: k < n // 2)


def scatter_dp(chunks, layer):
    n = lax.axis_size("dp")
    got = {k: over_dp(chunks[k], xor_pairs(n, k), layer) for k in reversed(range(1, n))}
    return [chunks[0]] + [got[k] for k in range(1, n)]


def down_a_section(chunks):
    n = lax.axis_size("tensor")
    m = lax.axis_size("layers")
    got = {
        k: lax.ppermute(
            chunks[k], ("tensor", "layers"), [(i * m + 1, j * m) for i, j in xor_pairs(n, k)]
        )
        for k in far_first(n)
    }
    got[0] = lax.ppermute(chunks[0], "layers", [(1, 0)])
    return [got[k] for k in range(n)]


def spread_halves(low, high, tensor_index):
    n = lax.axis_size("tensor")
    early = tensor_index < n // 2
    one = over_tensor(
        jnp.where(early, low, high),
        [(i, 2 * i if i < n // 2 else 2 * i + 1 - n) for i in range(n)],
        1,
    )
    two = over_tensor(
        jnp.where(early, high, low),
        [(i, 2 * i + 1 if i < n // 2 else 2 * i - n) for i in range(n)],
        1,
    )
    even = tensor_index % 2 == 0
    return jnp.where(even, one, two), jnp.where(even, two, one)


def whole(body, name, ins, outs, scratch=(), deps=()):
    arrays = [in_hbm(x) if m == pltpu.HBM else x for x, m in ins]
    specs = [pl.BlockSpec(memory_space=m) for _, m in ins]
    n_in, n_dep = len(arrays), len(deps)

    def run(*refs):
        body(*refs[:n_in], *refs[n_in + n_dep :])

    return pl.pallas_call(
        run,
        in_specs=specs + [pl.BlockSpec(memory_space=pl.ANY)] * n_dep,
        out_specs=[vspec()] * len(outs),
        out_shape=[jax.ShapeDtypeStruct(s, d) for s, d in outs],
        scratch_shapes=list(scratch),
        compiler_params=params(),
        name=name,
    )(*arrays, *deps)


def on_vmem(arrays):
    return [(x, pltpu.VMEM) for x in arrays]


def in_hbm(x):
    return pltpu.with_memory_space_constraint(x, pltpu.HBM)


def tile_width(width):
    return next(c for c in (512, 256, 128) if width % c == 0)


def tiles_of(width):
    tile = tile_width(width)
    return [slice(i, i + tile) for i in range(0, width, tile)]


def loads(src, dst, sems, count):
    rows = src.shape[0] // count
    return [
        pltpu.make_async_copy(
            src.at[pl.ds(c * rows, rows)], dst.at[pl.ds(c * rows, rows)], sems.at[c]
        )
        for c in range(count)
    ]


SPAN = 256


def span_of(size):
    return next(c for c in (SPAN, SPAN // 2) if size % c == 0)


def fill_hot(hot_s, at, row, base, span):
    width = row.shape[1]
    near = jnp.broadcast_to(row - base, (16, width)).astype(BF)
    step = lax.broadcasted_iota(jnp.int32, (16, width), 0).astype(F32)
    for i in range(0, span, 16):
        hit = (step + float(i)).astype(BF) == near
        hot_s[at + i : at + i + 16, :] = jnp.where(
            hit, jnp.ones((16, width), BF), jnp.zeros((16, width), BF)
        )


def prep_weights(lift_mask, proj_mask, lift, proj):
    steps = min(8, lift.shape[0] // BLK)

    def body(lift_mask_ref, proj_mask_ref, lift_h, proj_h, *refs):
        lift_out, proj_out, lift_s, proj_s, lift_sem, proj_sem = refs
        jobs = (
            (lift_mask_ref, lift_h, lift_out, lift_s, lift_sem),
            (proj_mask_ref, proj_h, proj_out, proj_s, proj_sem),
        )
        into = [loads(src, held, sem.at[0], steps) for _, src, _, held, sem in jobs]
        back = [loads(held, dst, sem.at[1], steps) for _, _, dst, held, sem in jobs]
        for i in range(steps):
            for copies in into:
                copies[i].start()
        for i in range(steps):
            for (mask, _, _, held, _), copies, stores in zip(jobs, into, back):
                copies[i].wait()
                n_rows = held.shape[0] // BLK // steps
                for r in range(i * n_rows, (i + 1) * n_rows):
                    for c in range(held.shape[1] // BLK):
                        at = (slice(r * BLK, (r + 1) * BLK), slice(c * BLK, (c + 1) * BLK))

                        @pl.when(mask[r, c] <= 0)
                        def _(held=held, at=at):
                            held[at] = jnp.zeros((BLK, BLK), BF)

                stores[i].start()
        for stores in back:
            for copy in stores:
                copy.wait()

    return pl.pallas_call(
        body,
        in_specs=[sspec(), sspec()] + [pl.BlockSpec(memory_space=pltpu.HBM)] * 2,
        out_specs=[pl.BlockSpec(memory_space=pltpu.HBM)] * 2,
        out_shape=[
            pltpu.HBM(lift.shape, BF),
            pltpu.HBM(proj.shape, BF),
        ],
        scratch_shapes=[
            pltpu.VMEM(lift.shape, BF),
            pltpu.VMEM(proj.shape, BF),
            pltpu.SemaphoreType.DMA((2, steps)),
            pltpu.SemaphoreType.DMA((2, steps)),
        ],
        compiler_params=params(),
        name="prep_weights",
    )(lift_mask, proj_mask, in_hbm(lift), in_hbm(proj))


def prep_inverse(perm, feat, deps):
    width = perm.shape[1]
    tile = tile_width(width)
    span = span_of(feat)

    def body(perm_ref, inv_ref, hot_s):
        lane = lax.broadcasted_iota(jnp.int32, (16, tile), 1)
        which = lax.broadcasted_iota(jnp.int32, (16, tile), 0)

        def step(s, _):
            base = s * span
            acc = jnp.zeros((16, span), F32)
            for c in range(width // tile):
                fill_hot(
                    hot_s, 0, perm_ref[:, c * tile : (c + 1) * tile], base.astype(F32), span
                )
                place = lane + (c * tile + 1)
                value = jnp.where(which == 0, place // 64, jnp.where(which == 1, place % 64, 0))
                acc = acc + dot_nt(value.astype(F32).astype(BF), hot_s[...])
            inv = acc[0:1, :] * 64.0 + acc[1:2, :] - 1.0
            inv_ref[:, pl.ds(pl.multiple_of(base, span), span)] = inv
            return 0

        lax.fori_loop(0, feat // span, step, 0)

    return whole(
        body,
        "prep_inverse",
        on_vmem([perm]),
        [((1, feat), F32)],
        [pltpu.VMEM((span, tile), BF)],
        deps=deps,
    )[0]


def forward(idx, tokens, perm, lift, proj, n, deps):
    rows, block = tokens[0].shape
    width = perm.shape[1]
    half, hid = lift.shape
    hb = half // n
    tile = tile_width(width)
    span = span_of(block)

    def body(idx_ref, *refs):
        tok = refs[:n]
        perm_ref, lift_h, proj_h, slope_ref, perm_s, hidden_ref = refs[n : n + 6]
        shared_out = refs[n + 6 : n + 6 + n]
        hot_s, lift_ref, proj_ref, lift_sem, proj_sem = refs[-5:]
        t = idx_ref[0]
        lift_in = loads(lift_h, lift_ref, lift_sem, n)
        proj_in = loads(proj_h, proj_ref, proj_sem, 2 * n)
        for copy in lift_in + proj_in:
            copy.start()

        def columns(c, _):
            cols = pl.ds(pl.multiple_of(c * tile, tile), tile)
            row = perm_ref[:, cols]
            acc = jnp.zeros((rows, tile), F32)
            for k in range(n):
                for i in range(0, block, span):
                    base = ((t ^ k) * block + i).astype(F32)
                    fill_hot(hot_s.at[k % 2], i, row, base, span)
                acc = acc + dot_nn(tok[k][...], hot_s[k % 2])
            perm_s[:, cols] = acc.astype(BF)
            return 0

        lax.fori_loop(0, width // tile, columns, 0)
        for copy in lift_in:
            copy.wait()
        for cols in tiles_of(hid):
            pre = dot_nn(perm_s[:, :half], lift_ref[:, cols])
            squash = sigmoid(pre)
            hidden_ref[:, cols] = (pre * squash).astype(BF)
            slope_ref[:, cols] = squash * (1.0 + pre * (1.0 - squash))
        hidden = hidden_ref[...]
        for copy in proj_in:
            copy.wait()
        for k in range(n):
            at = pl.multiple_of((t ^ k) * hb, hb)
            shared_out[k][:, :hb] = dot_nt(hidden, proj_ref[pl.ds(at, hb), :]).astype(BF)
            shared_out[k][:, hb:] = dot_nt(hidden, proj_ref[pl.ds(half + at, hb), :]).astype(BF)

    outs = whole(
        body,
        "forward",
        [(idx, pltpu.SMEM)]
        + on_vmem(list(tokens) + [perm])
        + [(lift, pltpu.HBM), (proj, pltpu.HBM)],
        [((rows, hid), F32), ((rows, width), BF), ((rows, hid), BF)]
        + [((rows, 2 * hb), BF)] * n,
        [
            pltpu.VMEM((2, block, tile), BF),
            pltpu.VMEM(lift.shape, BF),
            pltpu.VMEM(proj.shape, BF),
            pltpu.SemaphoreType.DMA((n,)),
            pltpu.SemaphoreType.DMA((2 * n,)),
        ],
        deps=deps,
    )
    return outs[0], outs[1], outs[2], outs[3:]


def bundles(idx, columns, hidden, half, n_dp):
    rows, hid = hidden.shape
    dpc = half // n_dp

    def body(idx_ref, columns_ref, hidden_ref, *refs):
        out, cond_s = refs[:n_dp], refs[n_dp]

        @pl.when(idx_ref[1] == 0)
        def _():
            fill_bundle(out, 0, columns_ref, hidden_ref, cond_s, idx_ref[2])

    return whole(
        body,
        "bundles",
        [(idx, pltpu.SMEM)] + on_vmem([columns, hidden]),
        [((rows, hid + dpc), BF)] * n_dp,
        [pltpu.VMEM((n_dp, rows, dpc), BF)],
    )


def fill_bundle(out, at, columns_ref, hidden_ref, cond_s, d):
    n_dp, _, dpc = cond_s.shape
    hid = hidden_ref.shape[1]
    for j in range(n_dp):
        cond_s[j] = columns_ref[:, j * dpc : (j + 1) * dpc]
    for k in range(n_dp):
        out[k][:, at : at + hid] = hidden_ref[...]
        out[k][:, at + hid : at + hid + dpc] = cond_s[d ^ k]


def couple(chunks, columns, half, cot, deps):
    n = len(chunks)
    n_cot = len(cot)
    rows, two_hb = chunks[0].shape
    hb = two_hb // 2

    def body(*refs):
        parts = refs[:n]
        cots = refs[n : n + n_cot]
        columns_ref, st_ref, log_ref = refs[n + n_cot :]
        raw = parts[0][:, :hb].astype(F32)
        shift = parts[0][:, hb:].astype(F32)
        for k in range(1, n):
            raw = raw + parts[k][:, :hb].astype(F32)
            shift = shift + parts[k][:, hb:].astype(F32)
        arg = raw + 2.0
        scale = sigmoid(arg)
        keep = 1.0 - scale
        cot = cots[0][...].astype(F32)
        for c in cots[1:]:
            cot = cot + c[...].astype(F32)
        cot = cot.astype(BF).astype(F32)
        grad_raw = cot * (columns_ref[:, half:].astype(F32) + shift) * scale * keep - keep
        st_ref[:, :hb] = grad_raw.astype(BF)
        st_ref[:, hb:] = (cot * scale).astype(BF)
        logs = jnp.minimum(arg, 0.0) - jnp.log(1.0 + jnp.exp(-jnp.abs(arg)))
        log_ref[...] = jnp.sum(logs, axis=0, keepdims=True)

    return whole(
        body,
        "couple",
        on_vmem(list(chunks) + list(cot) + [columns]),
        [((rows, two_hb), BF), ((1, hb), F32)],
        deps=deps,
    )


def fill_pack(pack, st_s, d, n_dp, m, hid, hb):
    for j in range(n_dp):
        for i in range(m):
            pack[j][:, hid + i * hb : hid + (i + 1) * hb] = st_s[(d ^ j) * m + i]


def order_st(st_ref, st_s, t, n, hb):
    for k in range(n):
        st_s[t ^ k] = st_ref[k][:, :hb]
        st_s[n + (t ^ k)] = st_ref[k][:, hb:]


def hidden_cotangent(st_s, slope_ref, proj_in, proj_ref, acc_s, out_ref, n, hb, hid):
    for k in range(2 * n):
        proj_in[k].wait()
        part = dot_nn(st_s[k], proj_ref[k * hb : (k + 1) * hb, :])
        if k == 0:
            acc_s[...] = part
        elif k + 1 < 2 * n:
            acc_s[...] += part
        else:
            out_ref[:, :hid] = ((acc_s[...] + part) * slope_ref[...]).astype(BF)


def mixed_part(pre, extra, shift_cot, lift_in, lift_ref, part_s, n, hb):
    for b in range(n):
        lift_in[b].wait()
        part = dot_nt(pre, lift_ref[b * hb : (b + 1) * hb, :])
        part_s[:, b * hb : (b + 1) * hb] = (part + extra(b)).astype(BF)
    part_s[:, n * hb :] = shift_cot


def natural_columns(part_ref, inv_ref, hots, first, count, hb, store):
    width = part_ref.shape[1]
    span = span_of(width)

    def two(i, _):
        for j, hot_s in enumerate(hots):
            q = first + 2 * i + j
            row = inv_ref[:, pl.ds(pl.multiple_of(q * hb, hb), hb)]
            for at in range(0, width, span):
                fill_hot(hot_s, at, row, float(at), span)
            store(q, dot_nn(part_ref[...], hot_s[...]).astype(BF))
        return 0

    lax.fori_loop(0, count // 2, two, 0)


def backward_one(idx, st, ca, slope, inv, lift, proj, width, n):
    rows, two_hb = st[0].shape
    hb = two_hb // 2
    hid = lift.shape[1]

    def body(idx_ref, *refs):
        st_ref = refs[:n]
        ca_ref, slope_ref, inv_ref, lift_h, proj_h = refs[n : n + 5]
        pre_ref, part_ref, nat_ref = refs[n + 5 : n + 8]
        second_out = refs[n + 8 : 2 * n + 8]
        st_s, acc_s, hot_a, hot_b, lift_ref, proj_ref, lift_sem, proj_sem = refs[-8:]
        t = idx_ref[0]
        proj_in = loads(proj_h, proj_ref, proj_sem, 2 * n)
        lift_in = loads(lift_h, lift_ref, lift_sem, n)
        for copy in proj_in + lift_in:
            copy.start()
        order_st(st_ref, st_s, t, n, hb)
        hidden_cotangent(st_s, slope_ref, proj_in, proj_ref, acc_s, pre_ref, n, hb, hid)
        mixed_part(
            pre_ref[...], lambda b: jnp.where(t == b, ca_ref[...].astype(F32), 0.0),
            st_ref[0][:, hb:], lift_in, lift_ref, part_ref, n, hb,
        )

        def store(q, block):
            nat_ref[q - n] = block

        natural_columns(part_ref, inv_ref, (hot_a, hot_b), n, n, hb, store)
        for k in range(n):
            second_out[k][...] = nat_ref[t ^ k]

    outs = whole(
        body,
        "backward_one",
        [(idx, pltpu.SMEM)]
        + on_vmem(list(st) + [ca, slope, inv])
        + [(lift, pltpu.HBM), (proj, pltpu.HBM)],
        [((rows, hid), BF), ((rows, width), BF), ((n, rows, hb), BF)] + [((rows, hb), BF)] * n,
        [
            pltpu.VMEM((2 * n, rows, hb), BF),
            pltpu.VMEM((rows, hid), F32),
            pltpu.VMEM((width, hb), BF),
            pltpu.VMEM((width, hb), BF),
            pltpu.VMEM(lift.shape, BF),
            pltpu.VMEM(proj.shape, BF),
            pltpu.SemaphoreType.DMA((n,)),
            pltpu.SemaphoreType.DMA((2 * n,)),
        ],
    )
    return outs[0], outs[1], outs[2], outs[3:]


def packs_one(idx, st, pre, columns, hidden, half, n_dp, deps):
    n = len(st)
    rows, two_hb = st[0].shape
    hb = two_hb // 2
    hid = pre.shape[1]
    m = 2 * n // n_dp
    dpc = half // n_dp

    def body(idx_ref, *refs):
        st_ref = refs[:n]
        pre_ref, columns_ref, hidden_ref = refs[n : n + 3]
        pack = refs[n + 3 : n + 3 + n_dp]
        st_s, cond_s = refs[-2:]

        @pl.when(idx_ref[1] != 0)
        def _():
            order_st(st_ref, st_s, idx_ref[0], n, hb)
            for j in range(n_dp):
                pack[j][:, :hid] = pre_ref[...]
            fill_pack(pack, st_s, idx_ref[2], n_dp, m, hid, hb)
            fill_bundle(pack, hid + m * hb, columns_ref, hidden_ref, cond_s, idx_ref[2])

    return whole(
        body,
        "packs_one",
        [(idx, pltpu.SMEM)] + on_vmem(list(st) + [pre, columns, hidden]),
        [((rows, 2 * hid + m * hb + dpc), BF)] * n_dp,
        [pltpu.VMEM((2 * n, rows, hb), BF), pltpu.VMEM((n_dp, rows, dpc), BF)],
        deps=deps,
    )


def backward_one_rest(idx, part, inv, n, deps):
    rows, width = part.shape
    hb = inv.shape[1] // (2 * n)

    def body(idx_ref, part_ref, inv_ref, nat_ref, *hot):
        @pl.when(idx_ref[1] != 0)
        def _():
            def store(q, block):
                nat_ref[q] = block

            natural_columns(part_ref, inv_ref, hot, 0, n, hb, store)

    return whole(
        body,
        "backward_one_rest",
        [(idx, pltpu.SMEM)] + on_vmem([part, inv]),
        [((n, rows, hb), BF)],
        [pltpu.VMEM((width, hb), BF)] * 2,
        deps=deps,
    )[0]


def backward_zero(idx, st, slope, proj, n, n_dp, deps):
    rows, two_hb = st[0].shape
    hb = two_hb // 2
    hid = proj.shape[1]
    m = 2 * n // n_dp

    def body(idx_ref, *refs):
        st_ref = refs[:n]
        slope_ref, proj_h = refs[n : n + 2]
        pack = refs[n + 2 : n + 2 + n_dp]
        st_s, acc_s, proj_ref, proj_sem = refs[-4:]

        @pl.when(idx_ref[1] == 0)
        def _():
            proj_in = loads(proj_h, proj_ref, proj_sem, 2 * n)
            for copy in proj_in:
                copy.start()
            order_st(st_ref, st_s, idx_ref[0], n, hb)
            hidden_cotangent(st_s, slope_ref, proj_in, proj_ref, acc_s, pack[0], n, hb, hid)
            for j in range(1, n_dp):
                pack[j][:, :hid] = pack[0][:, :hid]
            fill_pack(pack, st_s, idx_ref[2], n_dp, m, hid, hb)

    return whole(
        body,
        "backward_zero",
        [(idx, pltpu.SMEM)] + on_vmem(list(st) + [slope]) + [(proj, pltpu.HBM)],
        [((rows, hid + m * hb), BF)] * n_dp,
        [
            pltpu.VMEM((2 * n, rows, hb), BF),
            pltpu.VMEM((rows, hid), F32),
            pltpu.VMEM(proj.shape, BF),
            pltpu.SemaphoreType.DMA((2 * n,)),
        ],
        deps=deps,
    )


def natural_shares(idx, st_own, pack, low_one, inv, lift, low, high, width, n):
    rows, two_hb = st_own.shape
    hb = two_hb // 2
    hid = lift.shape[1]

    def body(idx_ref, st_ref, pack_ref, *refs):
        got_ref, inv_ref, lift_h, low_ref, high_ref = refs[:5]
        out = refs[5 : 5 + n]
        nat_s, part_s, hot_a, hot_b, lift_ref, lift_sem = refs[5 + n :]

        @pl.when(idx_ref[1] == 0)
        def _():
            lift_in = loads(lift_h, lift_ref, lift_sem, n)
            for copy in lift_in:
                copy.start()
            mixed_part(
                pack_ref[:, :hid], lambda b: got_ref[b].astype(F32), st_ref[:, hb:], lift_in,
                lift_ref, part_s, n, hb,
            )

            def store(q, block):
                nat_s[q] = block

            natural_columns(part_s, inv_ref, (hot_a, hot_b), 0, 2 * n, hb, store)

        @pl.when(idx_ref[1] != 0)
        def _():
            for q in range(n):
                nat_s[q] = low_ref[q]
                nat_s[n + q] = high_ref[q]

        for k in range(n):
            for q in range(2):
                out[k][:, q * hb : (q + 1) * hb] = nat_s[2 * (idx_ref[0] ^ k) + q]

    return whole(
        body,
        "natural_shares",
        [(idx, pltpu.SMEM)]
        + on_vmem([st_own, pack, low_one, inv])
        + [(lift, pltpu.HBM)]
        + on_vmem([low, high]),
        [((rows, 2 * hb), BF)] * n,
        [
            pltpu.VMEM((2 * n, rows, hb), BF),
            pltpu.VMEM((rows, width), BF),
            pltpu.VMEM((width, hb), BF),
            pltpu.VMEM((width, hb), BF),
            pltpu.VMEM(lift.shape, BF),
            pltpu.SemaphoreType.DMA((n,)),
        ],
    )


def fetch(idx_ref, kind, bund, zero, one, lhs, rhs, sem, wait):
    n_dp = len(one)
    rows = one[0].shape[0]
    hid = rhs.shape[1]
    width = lhs.shape[1]
    st_cols = zero[0].shape[1] - hid

    def act(src, first, dst, k, of):
        copy = pltpu.make_async_copy(
            src.at[:, pl.ds(first, dst.shape[1])],
            dst.at[pl.ds(k * rows, rows)],
            sem.at[of * n_dp + k],
        )
        if wait:
            copy.wait()
        else:
            copy.start()

    def act_all(pack, late, late_at):
        for k in range(n_dp):
            if kind == "proj":
                act(pack[k], hid, lhs, k, 0)
                act(late[k], late_at, rhs, k, 1)
            else:
                act(late[k], late_at + hid, lhs, k, 0)
                act(pack[k], 0, rhs, k, 1)

    @pl.when(idx_ref[1] == 0)
    def _():
        act_all(zero, bund, 0)

    @pl.when(idx_ref[1] != 0)
    def _():
        act_all(one, one, hid + st_cols)


def factors(kind, bund, zero, hid):
    n_dp = len(zero)
    tokens = n_dp * zero[0].shape[0]
    width = (zero if kind == "proj" else bund)[0].shape[1] - hid
    return [
        pltpu.VMEM((tokens, width), BF),
        pltpu.VMEM((tokens, hid), BF),
        pltpu.SemaphoreType.DMA((2 * n_dp,)),
    ]


def weight_squares(idx, lift_mask, proj_mask, bund, zero, one, logs_zero, logs_one, hid, deps):
    n_dp = len(zero)
    lift_s = factors("lift", bund, zero, hid)
    proj_s = factors("proj", bund, zero, hid)

    def body(idx_ref, lift_mask_ref, proj_mask_ref, log_zero_ref, log_one_ref, *refs):
        packs = [refs[i * n_dp : (i + 1) * n_dp] for i in range(3)]
        refs = refs[3 * n_dp :]
        sum_ref, sq_s = refs[:2]
        groups = (("proj", proj_mask_ref, refs[2:5]), ("lift", lift_mask_ref, refs[5:8]))
        for kind, _, (lhs, rhs, sem) in groups:
            fetch(idx_ref, kind, *packs, lhs, rhs, sem, False)
        sq_s[...] = jnp.zeros_like(sq_s)
        d = idx_ref[2]
        for kind, mask, (lhs, rhs, sem) in groups:
            fetch(idx_ref, kind, *packs, lhs, rhs, sem, True)
            n_rows = lhs.shape[1]
            first = d * (n_rows // BLK)
            tile = min(512, n_rows)
            for cols in tiles_of(hid):
                for r in range(0, n_rows, tile):
                    grad = dot_tn(lhs[:, r : r + tile], rhs[:, cols])
                    total = None
                    for i in range(grad.shape[0] // BLK):
                        for j in range(grad.shape[1] // BLK):
                            part = grad[i * BLK : (i + 1) * BLK, j * BLK : (j + 1) * BLK]
                            kept = mask[first + r // BLK + i, cols.start // BLK + j] > 0
                            part = jnp.sum((part * part).reshape(BLK // 8, 8, BLK), axis=0)
                            part = jnp.where(kept, part, 0.0)
                            total = part if total is None else total + part
                    sq_s[...] += total
        lane = lax.broadcasted_iota(jnp.int32, sum_ref.shape, 1)
        square = jnp.sum(sq_s[...])
        log_sum = jnp.sum(jnp.where(idx_ref[1] == 0, log_zero_ref[...], log_one_ref[...]))
        sum_ref[...] = jnp.where(lane == 0, square, jnp.where(lane == 1, log_sum, 0.0))

    n_all = lax.axis_size("dp") * lax.axis_size("tensor") * lax.axis_size("layers")
    return whole(
        body,
        "weight_squares",
        [(idx, pltpu.SMEM), (lift_mask, pltpu.SMEM), (proj_mask, pltpu.SMEM)]
        + on_vmem([logs_zero, logs_one])
        + [(x, pltpu.HBM) for x in list(bund) + list(zero) + list(one)],
        [((n_all, BLK), F32)],
        [pltpu.VMEM((8, BLK), F32)] + proj_s + lift_s,
        deps=deps,
    )[0]


def adam(idx, sums, masks, sources, moments, squares, hid, dep, log_count):
    n_dp = len(sources[0])
    n_cols = moments[0].shape[1]
    tile = min(2 * BLK, *(x.shape[0] for x in moments))
    counts = [x.shape[0] // tile for x in moments]
    firsts = (0, counts[0])
    steps = sum(counts)
    kinds = ("proj", "lift")
    n_layers = lax.axis_size("layers")
    inv_one = 1.0 / (1.0 - beta_one**ADAM_STEP)
    inv_two = 1.0 / (1.0 - beta_two**ADAM_STEP)

    def body(idx_ref, proj_mask_ref, lift_mask_ref, sums_ref, dep_ref, *refs):
        packs = [refs[i * n_dp : (i + 1) * n_dp] for i in range(3)]
        refs = refs[3 * n_dp :]
        states = (refs[0:2], refs[2:4])
        outs = (refs[4:7], refs[7:10])
        log_ref = refs[10]
        scratch = (refs[11:14], refs[14:17])
        held = refs[17:20]
        load_sem, store_sem = refs[20:22]
        masks_ref = (proj_mask_ref, lift_mask_ref)

        def rows_of(i):
            return pl.ds(pl.multiple_of(i * tile, tile), tile)

        def load(which, i):
            return [
                pltpu.make_async_copy(
                    states[which][j].at[rows_of(i)],
                    held[j].at[rows_of(firsts[which] + i)],
                    load_sem.at[j, firsts[which] + i],
                )
                for j in range(2)
            ]

        def store(which, i):
            return [
                pltpu.make_async_copy(
                    held[j].at[rows_of(firsts[which] + i)],
                    outs[which][j].at[rows_of(i)],
                    store_sem.at[j, firsts[which] + i],
                )
                for j in range(3)
            ]

        for which, (kind, (lhs, rhs, sem)) in enumerate(zip(kinds, scratch)):
            fetch(idx_ref, kind, *packs, lhs, rhs, sem, False)
            for i in range(counts[which]):
                for copy in load(which, i):
                    copy.start()
        square_total = jnp.sum(sums_ref[:, 0:1], axis=0, keepdims=True)
        factor = jnp.minimum(1.0, CLIP / (jnp.sqrt(square_total) + 1e-06))
        place = lax.broadcasted_iota(jnp.int32, sums_ref.shape, 0) % n_layers
        lane = lax.broadcasted_iota(jnp.int32, sums_ref.shape, 1)
        own_log = (place == idx_ref[1]) & (lane == 1)
        log_ref[0] = jnp.sum(jnp.where(own_log, sums_ref[...], 0.0)) / log_count
        for which in range(2):
            lhs, rhs, sem = scratch[which]
            mask_ref = masks_ref[which]
            fetch(idx_ref, kinds[which], *packs, lhs, rhs, sem, True)

            def update(i, _, which=which, lhs=lhs, rhs=rhs, mask_ref=mask_ref):
                for copy in load(which, i):
                    copy.wait()
                row = (idx_ref[2] * counts[which] + i) * (tile // BLK)
                rows = rows_of(firsts[which] + i)
                left = lhs[:, rows_of(i)]
                for cols in tiles_of(n_cols):
                    grad = dot_tn(left, rhs[:, cols])
                    for r in range(tile // BLK):
                        sub = pl.ds(pl.multiple_of(rows.start + r * BLK, BLK), BLK)
                        for j in range(grad.shape[1] // BLK):
                            first_col = cols.start + j * BLK
                            at = (sub, slice(first_col, first_col + BLK))
                            kept = mask_ref[row + r, first_col // BLK] > 0
                            g = grad[r * BLK : (r + 1) * BLK, j * BLK : (j + 1) * BLK] * factor
                            old_m, old_v = held[0][at], held[1][at]
                            new_m = beta_one * old_m + (1.0 - beta_one) * g
                            new_v = beta_two * old_v + (1.0 - beta_two) * g * g
                            spread = new_v * inv_two
                            upd = (new_m * inv_one) / (spread * lax.rsqrt(spread) + adam_eps)
                            held[0][at] = jnp.where(kept, new_m, old_m)
                            held[1][at] = jnp.where(kept, new_v, old_v)
                            held[2][at] = jnp.where(kept, upd, 0.0)
                for copy in store(which, i):
                    copy.start()
                return 0

            lax.fori_loop(0, counts[which], update, 0)
        for which in range(2):
            for i in range(counts[which]):
                for copy in store(which, i):
                    copy.wait()

    operands = [in_hbm(x) for group in sources for x in group]
    states = [in_hbm(x) for pair in zip(moments, squares) for x in pair]
    hbm = pl.BlockSpec(memory_space=pltpu.HBM)
    return pl.pallas_call(
        body,
        in_specs=[sspec()] * 3
        + [vspec()]
        + [pl.BlockSpec(memory_space=pl.ANY)]
        + [hbm] * (3 * n_dp + 4),
        out_specs=[hbm] * 6 + [sspec()],
        out_shape=[pltpu.HBM(x.shape, F32) for x in moments for _ in range(3)]
        + [jax.ShapeDtypeStruct((1,), F32)],
        scratch_shapes=[x for kind in kinds for x in factors(kind, sources[0], sources[1], hid)]
        + [pltpu.VMEM((steps * tile, n_cols), F32)] * 3
        + [pltpu.SemaphoreType.DMA((2, steps)), pltpu.SemaphoreType.DMA((3, steps))],
        compiler_params=pltpu.CompilerParams(vmem_limit_bytes=28 * 1024 * 1024),
        name="adam",
    )(idx, *masks, sums, dep, *operands, *states)


def total(parts):
    acc = parts[0].astype(F32)
    for p in parts[1:]:
        acc = acc + p.astype(F32)
    return acc


def per_device(
    section_input,
    out_cotangent,
    lift_weight,
    proj_weight,
    lift_mask,
    proj_mask,
    channel_perm,
    lift_moment,
    lift_square,
    proj_moment,
    proj_square,
):
    n = lax.axis_size("tensor")
    n_dp = lax.axis_size("dp")
    t = lax.axis_index("tensor")
    section = lax.axis_index("layers")
    d = lax.axis_index("dp")
    idx = jnp.stack([t, section, d]).astype(jnp.int32)
    perm = channel_perm[0]
    feat = perm.shape[0]
    half = feat // 2
    hb = half // n
    rows = section_input.shape[1]
    lift_mask, proj_mask = lift_mask[0], proj_mask[0]

    with jax.named_scope("tokens_exchange"):
        tokens = gather_tensor(section_input[0], None)
    with jax.named_scope("cotangent_exchange"):
        ca, cb = spread_halves(out_cotangent[:, :hb], out_cotangent[:, hb:], t)

    own = lax.dynamic_slice_in_dim(perm, half + t * hb, hb, 0)
    perm_cols = jnp.concatenate([perm[:half], own])[None].astype(F32)
    width = perm_cols.shape[1]
    hid = lift_weight.shape[2]
    lift, proj = prep_weights(lift_mask, proj_mask, lift_weight[0], proj_weight[0])

    slope, columns, hidden, shared = forward(
        idx, tokens, perm_cols, lift, proj, n, (ca, cb)
    )
    with jax.named_scope("shared_exchange"):
        shared = scatter_tensor(shared, None)
    with jax.named_scope("hidden_exchange"):
        bund = scatter_dp(bundles(idx, columns, hidden, half, n_dp), 0)
    inv = prep_inverse(perm_cols, feat, (columns,))

    st_own, logs_one = couple(shared, columns, half, [cb], (inv,) + tuple(bund[1:]))
    with jax.named_scope("st_one_exchange"):
        st = gather_tensor(st_own, 1)
    pre, part, high, second = backward_one(idx, st, ca, slope, inv, lift, proj, width, n)
    with jax.named_scope("down_exchange"):
        cb_zero = down_a_section(second)

    st_own, logs_zero = couple(shared, columns, half, cb_zero[::-1], ())
    with jax.named_scope("st_zero_exchange"):
        st_zero = gather_tensor(st_own, 0)
    pack_zero = backward_zero(idx, st_zero, slope, proj, n, n_dp, ())
    with jax.named_scope("dp_zero_exchange"):
        pack_got = scatter_dp(pack_zero, 0)
    pack_one = packs_one(idx, st, pre, columns, hidden, half, n_dp, (pack_zero[0],))
    with jax.named_scope("dp_one_exchange"):
        pack_one = scatter_dp(pack_one, 1)
    low = backward_one_rest(idx, part, inv, n, tuple(pack_one[1:]))
    with jax.named_scope("down_late_exchange"):
        low_one = lax.ppermute(low, "layers", [(1, 0)])
    shares = natural_shares(
        idx, st_own, pack_zero[0], low_one, inv, lift, low, high, width, n
    )

    order = [0] + list(reversed(range(1, n_dp)))
    sources = tuple([group[k] for k in order] for group in (bund, pack_got, pack_one))
    sums = weight_squares(idx, lift_mask, proj_mask, *sources, logs_zero, logs_one, hid, tuple(shares))
    with jax.named_scope("norm_exchange"):
        sums = lax.all_to_all(
            sums, ("dp", "tensor", "layers"), split_axis=0, concat_axis=0, tiled=True
        )
    with jax.named_scope("input_exchange"):
        got = scatter_tensor(shares, None)
    updated = adam(
        idx,
        sums,
        (proj_mask, lift_mask),
        sources,
        (proj_moment[0], lift_moment[0]),
        (proj_square[0], lift_square[0]),
        hid,
        shares[0],
        rows * n_dp * half,
    )
    proj_out, lift_out, log_det = updated[:3], updated[3:6], updated[6]

    input_grad = total(got)[None]
    return (
        input_grad,
        log_det,
        lift_out[0][None],
        lift_out[1][None],
        lift_out[2][None],
        proj_out[0][None],
        proj_out[1][None],
        proj_out[2][None],
    )


def solution(mesh):
    return jax.shard_map(
        per_device,
        mesh=mesh,
        in_specs=(
            P("layers", "dp", "tensor"),
            P("dp", "tensor"),
            P("layers", None, "tensor"),
            P("layers", None, "tensor"),
            P("layers", None, "tensor"),
            P("layers", None, "tensor"),
            P("layers", None),
            P("layers", "dp", "tensor"),
            P("layers", "dp", "tensor"),
            P("layers", "dp", "tensor"),
            P("layers", "dp", "tensor"),
        ),
        out_specs=(
            P("layers", "dp", "tensor"),
            P("layers"),
            P("layers", "dp", "tensor"),
            P("layers", "dp", "tensor"),
            P("layers", "dp", "tensor"),
            P("layers", "dp", "tensor"),
            P("layers", "dp", "tensor"),
            P("layers", "dp", "tensor"),
        ),
        check_vma=False,
    )
```
